32 devices in a mesh: px: 4 (over z), py: 8 (over y, x, core).
Axes of the slice: x: 2, y: 2, z: 4, core: 2. Of those that a mesh axis runs over, the one named last changes fastest.
Arguments:
- fractions: float32 [1024, 3, 128], P(('px', 'py')), may hold values from 0 to 1
- charge: float32 [1024, 128], P(('px', 'py')), may hold values from -4 to 4
- cell_index: int32 [1024, 128], P(('px', 'py')), may hold values from 0 to 524287
- destination: int32 [1024, 1], P(('px', 'py')), may hold values from 0 to 7; in each aligned block of 32 rows (0 to 31, 32 to 63, ...) at most 6 rows name the same one
- live_blocks: int32 [32], P(('px', 'py')), may hold values from 16 to 32, as said below
Outputs:
- forces: float32 [1024, 3, 128], P(('px', 'py'))
The draws below stay inside these ranges and needn't reach their ends.
Inputs may be any that keep to these rules, and one draw needn't show every extreme that they name: `destination`: in the rows of one device no value is named by more than 6 blocks, a bound that some block reaches. `live_blocks`: some domain has all 32 slots occupied in every draw.
All inputs are finite; a program needn't handle non-finite values.
Results may differ from the reference program's by a relative error of at most 0.0003.
Values sent between devices are 32-bit elements; how exact they have to be, the bound alone decides.
A program may use at most 128 MiB of HBM per device.

```python
import math
import jax
import jax.numpy as jnp
import numpy as np

K = 256
BLOCK_ROWS = 128
BLK_DEV = 32
CX = 64
CY = 32
CAP = 6
NBLK = 1024
N_PX = 4
N_PY = 8


def draw_live_blocks(key, part):
    counts = jax.random.randint(key, (N_PX * N_PY,), BLK_DEV // 2, BLK_DEV + 1)
    chosen = jax.random.randint(jax.random.fold_in(key, 7), (), 0, N_PX * N_PY)
    return jnp.where(jnp.arange(N_PX * N_PY) == chosen, BLK_DEV, counts).astype(jnp.int32)


def plant(values, own_key, low, largest):
    longest = values.shape.index(max(values.shape))
    spots = []
    for shift in (0, 1):
        where = [jax.random.randint(jax.random.fold_in(own_key, axis), (), 0, length) for axis, length in enumerate(values.shape)]
        where[longest] = (where[longest] + shift) % values.shape[longest]
        spots.append(tuple(where))
    return values.at[spots[0]].set(low).at[spots[1]].set(largest)


def block_levels(own_key, shape, pieces, smallest, top_value):
    factor_of, own = 1.0, jax.random.fold_in(own_key, 6)
    for position, blocks in pieces:
        draws = jnp.exp(jax.random.uniform(jax.random.fold_in(own, position), (blocks,), jnp.float32, smallest / len(pieces), top_value / len(pieces)))
        factor_of = factor_of * jnp.repeat(draws, shape[position] // blocks).reshape([-1 if axis == position else 1 for axis in range(len(shape))])
    return factor_of


def shared_out(rng, own, number, rows, number_of, top, reach, lean):
    order = jax.random.permutation(rng, number_of)
    heavy_load, common = shares(number_of, rows * top, reach, lean, True), shares(number_of, rows * top, reach, lean, False)
    places = jnp.arange(number_of)

    def named(sizes, turn):
        used = int((sizes > 0).sum())
        fixed = max(1, used // 4)
        passed = fixed + (places - fixed + turn * (used - fixed)) % max(1, number_of - fixed)
        return jnp.zeros((number_of,), jnp.int32).at[order[jnp.where(places < fixed, places, passed)]].set(jnp.asarray(sizes, jnp.int32))

    sizes = jnp.where(number % 4 == 0, named(heavy_load, number // 4), named(common, number - number // 4 - 1))
    mixed = jax.random.permutation(jax.random.fold_in(own, 3), number_of)
    source_of, taker = mixed[0:number_of // 2 * 2:2], mixed[1:number_of // 2 * 2:2]
    room = jnp.minimum(sizes[source_of] - 1, reach - sizes[taker]) // 2
    room = jnp.where((source_of == order[0]) | (taker == order[0]) | (sizes[taker] == 0), 0, jnp.maximum(room, 0))
    passed = jax.random.randint(jax.random.fold_in(own, 4), (number_of // 2,), 0, 1 << 20) % (room + 1)
    sizes = sizes.at[source_of].add(-passed).at[taker].add(passed)
    labels = jnp.searchsorted(jnp.cumsum(sizes), jnp.arange(rows * top), side="right").astype(jnp.int32)
    table = labels.reshape(top, rows).T
    table = table[jax.random.permutation(jax.random.fold_in(own, 1), rows)]
    turn = jax.random.randint(jax.random.fold_in(own, 2), (rows, 1), 0, top)
    return jnp.take_along_axis(table, (jnp.arange(top)[None, :] + turn) % top, axis=1)


def shares(number_of, total, limit, skew, full):
    loads = [(1 << 20) // math.isqrt(rank ** skew) + 1 for rank in range(1, number_of + 1)]
    largest = limit if full else min(limit, max(-(-total // number_of), total * loads[0] // sum(loads)))
    least = 1 if total - largest >= number_of - 1 else 0
    holding, spare = [largest] + [least] * (number_of - 1), total - largest - least * (number_of - 1)
    while spare > 0:
        candidates = [i for i in range(1, number_of) if holding[i] < largest] or [i for i in range(1, number_of) if holding[i] < limit]
        pool, budget = sum([loads[i] for i in candidates]), spare
        for i in candidates:
            extra = min(limit - holding[i], max(1, budget * loads[i] // pool), spare)
            holding[i] = holding[i] + extra
            spare = spare - extra
    return np.array(holding)


def centred(own_key, shape, width, most, split=(), kind=jnp.bfloat16):
    entries = jax.random.normal(own_key, shape, jnp.float32) * width
    if len(split) > 0:
        entries = block_levels(own_key, shape, split, -0.22, 0.18) * entries
    return jnp.clip(entries, min=-most, max=most).astype(kind)


def setup_inputs(seed: int = 0) -> dict:
    seeds = jax.random.split(jax.random.key(seed), 6)
    fractions = jnp.clip(1.0 * jax.random.uniform(seeds[0], (NBLK, 3, BLOCK_ROWS), jnp.float32) ** block_levels(seeds[0], (NBLK, 3, BLOCK_ROWS), ((0, 32),), -0.2, 0.2), 0.0, 1.0)
    charge = centred(seeds[1], (NBLK, BLOCK_ROWS), 1.0, 4.0, ((0, 32),), jnp.float32)
    cell_index = plant(jax.random.randint(seeds[2], (NBLK, BLOCK_ROWS), 0, CX * CY * K), jax.random.fold_in(seeds[2], 1), 0, (CX * CY * K) - 1).astype(jnp.int32)
    destination_keys = jax.random.split(jax.random.fold_in(seeds[3], 1), NBLK // BLK_DEV)
    destination_turns = jax.random.permutation(jax.random.fold_in(seeds[3], 3), NBLK // BLK_DEV)
    destination = jax.vmap(lambda own, number: shared_out(jax.random.fold_in(seeds[3], 2), own, number, BLK_DEV, N_PY, 1, CAP, 2))(destination_keys, destination_turns).reshape((NBLK, 1))
    live_blocks = draw_live_blocks(jax.random.fold_in(seeds[5], 71), 0)
    return {"fractions": fractions, "charge": charge, "cell_index": cell_index, "destination": destination, "live_blocks": live_blocks}


EWALD_GAIN = 4.0
EWALD_BETA = 0.6
SPLINE_SUMS = (1.0 / 120.0, 26.0 / 120.0, 66.0 / 120.0, 26.0 / 120.0, 1.0 / 120.0)


def spline_six(u):
    older_values = [1.0 - u, u]
    slopes = []
    for spline_order in range(3, 7):
        newer_values = []
        for k in range(spline_order):
            from_left = older_values[k - 1] if k >= 1 else jnp.zeros_like(u)
            from_right = older_values[k] if k <= spline_order - 2 else jnp.zeros_like(u)
            newer_values.append(((u + (spline_order - 1 - k)) * from_left + (k + 1 - u) * from_right) * (1.0 / (spline_order - 1)))
        if spline_order == 6:
            slopes = [(older_values[k - 1] if k >= 1 else jnp.zeros_like(u)) - (older_values[k] if k <= 4 else jnp.zeros_like(u)) for k in range(6)]
        older_values = newer_values
    return older_values, slopes


def modulus(wave, extent):
    cos_sum = jnp.zeros(wave.shape, jnp.float32)
    sin_sum = jnp.zeros(wave.shape, jnp.float32)
    for j, value in enumerate(SPLINE_SUMS):
        angle = (2.0 * math.pi / extent) * ((wave * j) % extent).astype(jnp.float32)
        cos_sum = cos_sum + value * jnp.cos(angle)
        sin_sum = sin_sum + value * jnp.sin(angle)
    return 1.0 / (cos_sum * cos_sum + sin_sum * sin_sum)


def influence(wave_x, wave_y, wave_z, extent):
    folded_x = jnp.where(2 * wave_x < extent, wave_x, wave_x - extent).astype(jnp.float32) / extent
    folded_y = jnp.where(2 * wave_y < extent, wave_y, wave_y - extent).astype(jnp.float32) / extent
    folded_z = jnp.where(2 * wave_z < extent, wave_z, wave_z - extent).astype(jnp.float32) / extent
    squared = folded_x * folded_x + folded_y * folded_y + folded_z * folded_z
    safe_squared = jnp.where(squared > 0, squared, 1.0)
    value = EWALD_GAIN * jnp.exp(-(math.pi * math.pi) * squared / (EWALD_BETA * EWALD_BETA)) / safe_squared
    value = value * modulus(wave_x, extent) * modulus(wave_y, extent) * modulus(wave_z, extent)
    return jnp.where(squared > 0, value, 0.0)


def reference(fractions, charge, cell_index, destination, live_blocks):
    block_ids = jnp.arange(NBLK, dtype=jnp.int32)
    device_ids = block_ids // BLK_DEV
    alive = (block_ids % BLK_DEV < live_blocks[device_ids]).astype(jnp.float32)
    row_part = device_ids // N_PY
    amounts = (charge * alive[:, None]).reshape(-1)
    cells_flat = cell_index.reshape(-1)
    grid_x = jnp.repeat(row_part, BLOCK_ROWS) * CX + cells_flat // (CY * K)
    grid_y = jnp.repeat(destination[:, 0], BLOCK_ROWS) * CY + (cells_flat // K) % CY
    grid_z = cells_flat % K
    splines_x, slopes_x = spline_six(fractions[:, 0, :].reshape(-1))
    splines_y, slopes_y = spline_six(fractions[:, 1, :].reshape(-1))
    splines_z, slopes_z = spline_six(fractions[:, 2, :].reshape(-1))
    along_z = jnp.stack(splines_z, axis=1)
    slope_z = jnp.stack(slopes_z, axis=1)
    z_index = (grid_z[:, None] + jnp.arange(6, dtype=jnp.int32)[None, :]) % K
    density = jnp.zeros((K, K, K), jnp.float32)
    for a in range(6):
        for b in range(6):
            x_index = (grid_x + a) % K
            y_index = (grid_y + b) % K
            amount = (amounts * splines_x[a] * splines_y[b])[:, None] * along_z
            density = density.at[x_index[:, None], y_index[:, None], z_index].add(amount)
    spectrum = jnp.fft.fftn(density)
    waves = jnp.arange(K, dtype=jnp.int32)
    kernel = influence(waves[:, None, None], waves[None, :, None], waves[None, None, :], K)
    potential = jnp.real(jnp.fft.ifftn(spectrum * kernel)).astype(jnp.float32)
    force_x = jnp.zeros(amounts.shape, jnp.float32)
    force_y = jnp.zeros(amounts.shape, jnp.float32)
    force_z = jnp.zeros(amounts.shape, jnp.float32)
    for a in range(6):
        for b in range(6):
            x_index = (grid_x + a) % K
            y_index = (grid_y + b) % K
            values = potential[x_index[:, None], y_index[:, None], z_index]
            plain = jnp.sum(values * along_z, axis=1)
            sloped = jnp.sum(values * slope_z, axis=1)
            force_x = force_x + slopes_x[a] * splines_y[b] * plain
            force_y = force_y + splines_x[a] * slopes_y[b] * plain
            force_z = force_z + splines_x[a] * splines_y[b] * sloped
    forces = -amounts[None, :] * jnp.stack([force_x, force_y, force_z])
    return forces.reshape(3, NBLK, BLOCK_ROWS).transpose(1, 0, 2)
```

```python
import math

import jax
import jax.numpy as jnp
import numpy as np
from jax import lax
from jax.experimental import pallas as pl
from jax.experimental.pallas import tpu as pltpu
from jax.sharding import PartitionSpec as P

K = 256
EWALD_GAIN = 4.0
EWALD_BETA = 0.6
SPLINE_SUMS = (1.0 / 120.0, 26.0 / 120.0, 66.0 / 120.0, 26.0 / 120.0, 1.0 / 120.0)
HIGHEST = lax.Precision.HIGHEST
HIGH = lax.Precision.HIGH
LANES = 128
ROWS_CHUNK = 14
GROUP_BLOCKS = 2


def hartley():
    steps = np.arange(K)
    angle = 2.0 * math.pi / K * (np.outer(steps, steps) % K)
    return (np.cos(angle) + np.sin(angle)).astype(np.float32)


def wave_profile():
    steps = np.arange(K)
    folded = np.where(2 * steps < K, steps, steps - K) / K
    waves = np.exp(2j * math.pi / K * np.outer(steps, np.arange(5)))
    modulus = 1.0 / np.abs(waves @ np.array(SPLINE_SUMS)) ** 2
    squared = folded * folded
    gauss = np.exp(-(math.pi * math.pi) * squared / (EWALD_BETA * EWALD_BETA))
    return squared.astype(np.float32), (gauss * modulus).astype(np.float32)


def from_behind(value, axis, steps):
    count = lax.axis_size(axis)
    pairs = [(source, (source + steps) % count) for source in range(count)]
    return lax.ppermute(value, axis, pairs)


def spline_six(u):
    older_values = [1.0 - u, u]
    slopes = []
    for spline_order in range(3, 7):
        newer_values = []
        for k in range(spline_order):
            terms = []
            if k >= 1:
                terms.append((u + (spline_order - 1 - k)) * older_values[k - 1])
            if k <= spline_order - 2:
                terms.append((k + 1 - u) * older_values[k])
            newer_values.append(sum(terms[1:], terms[0]) * (1.0 / (spline_order - 1)))
        if spline_order == 6:
            slopes = [-older_values[0]]
            slopes += [older_values[k - 1] - older_values[k] for k in range(1, 5)]
            slopes += [older_values[4]]
        older_values = newer_values
    return (older_values, slopes)


def placed(offset, values):
    table = jnp.zeros(offset.shape, jnp.float32)
    for k in range(6):
        table = jnp.where(offset == k, values[k], table)
    return table


def offsets(base, rows, wrap):
    width = base.shape[1]
    offset = lax.broadcasted_iota(jnp.int32, (rows, width), 0) - base
    return offset & (K - 1) if wrap else offset


def halves(value):
    upper = value.astype(jnp.bfloat16)
    lower = (value - upper.astype(jnp.float32)).astype(jnp.bfloat16)
    return upper, lower


def deposit_kernel(count_ref, atoms_ref, grid_ref):
    step = pl.program_id(0)
    rows, columns, depth = grid_ref.shape
    width = atoms_ref.shape[2]

    @pl.when(step == 0)
    def _():
        grid_ref[...] = jnp.zeros(grid_ref.shape, jnp.float32)

    @pl.when(step < count_ref[0])
    def _():
        atoms = atoms_ref[0]
        base = atoms.astype(jnp.int32)
        table_x = placed(offsets(base[4:5], rows, False), spline_six(atoms[0:1])[0])
        table_y = placed(offsets(base[5:6], columns, False), spline_six(atoms[1:2])[0])
        table_z = placed(offsets(base[6:7], depth, True), spline_six(atoms[2:3])[0])
        upper, lower = halves((table_z * atoms[3:4]).T)
        weights = jnp.concatenate([upper, lower, upper], axis=0)
        for start in range(0, rows, ROWS_CHUNK):
            chunk = table_x[start : start + ROWS_CHUNK]
            outer = (chunk[:, None, :] * table_y[None, :, :]).reshape(-1, width)
            upper, lower = halves(outer)
            spread = jnp.dot(
                jnp.concatenate([upper, upper, lower], axis=1),
                weights,
                preferred_element_type=jnp.float32,
            )
            grid_ref[start : start + ROWS_CHUNK] += spread.reshape(-1, columns, depth)


def pull_kernel(count_ref, atoms_ref, potential_ref, forces_ref, parts):
    step = pl.program_id(0)
    rows, columns, depth = potential_ref.shape
    width = atoms_ref.shape[2]
    piece = ROWS_CHUNK * columns

    @pl.when(step == 0)
    def _():
        for index in range(rows // ROWS_CHUNK):
            start = index * ROWS_CHUNK
            values = potential_ref[start : start + ROWS_CHUNK].reshape(piece, depth)
            upper, lower = halves(values)
            parts[index * piece : (index + 1) * piece] = jnp.concatenate(
                [upper, lower, upper], axis=1
            )

    @pl.when(step >= count_ref[0])
    def _():
        forces_ref[...] = jnp.zeros(forces_ref.shape, jnp.float32)

    @pl.when(step < count_ref[0])
    def _():
        atoms = atoms_ref[0]
        base = atoms.astype(jnp.int32)
        offset_x = offsets(base[4:5], rows, False)
        offset_y = offsets(base[5:6], columns, False)
        offset_z = offsets(base[6:7], depth, True)
        values, slopes = spline_six(atoms[0:1])
        table_x, slope_x = placed(offset_x, values), placed(offset_x, slopes)
        values, slopes = spline_six(atoms[1:2])
        table_y, slope_y = placed(offset_y, values), placed(offset_y, slopes)
        values, slopes = spline_six(atoms[2:3])
        both = jnp.concatenate([placed(offset_z, values), placed(offset_z, slopes)], axis=1)
        upper, lower = halves(both)
        weights = jnp.concatenate([upper, upper, lower], axis=0)
        totals = [jnp.zeros((8, width), jnp.float32) for _ in range(3)]
        for index in range(rows // ROWS_CHUNK):
            start = index * ROWS_CHUNK
            sampled = jnp.dot(
                parts[index * piece : (index + 1) * piece],
                weights,
                preferred_element_type=jnp.float32,
            ).reshape(ROWS_CHUNK, columns, 2 * width)
            for row in range(ROWS_CHUNK):
                plain = sampled[row, :, :width]
                sloped = sampled[row, :, width:]
                value_x = table_x[start + row : start + row + 1]
                turned_x = slope_x[start + row : start + row + 1]

                def folded(terms):
                    return jnp.sum(terms.reshape(columns // 8, 8, width), axis=0)

                totals[0] = totals[0] + turned_x * folded(plain * table_y)
                totals[1] = totals[1] + value_x * folded(plain * slope_y)
                totals[2] = totals[2] + value_x * folded(sloped * table_y)
        result = [-atoms[3:4] * jnp.sum(total, axis=0, keepdims=True) for total in totals]
        forces_ref[0] = jnp.concatenate(
            result + [jnp.zeros((5, width), jnp.float32)], axis=0
        )


def deposit(count, atoms, rows, columns):
    groups, lines, width = atoms.shape
    return pl.pallas_call(
        deposit_kernel,
        out_shape=jax.ShapeDtypeStruct((rows, columns, K), jnp.float32),
        grid=(groups,),
        in_specs=[
            pl.BlockSpec(memory_space=pltpu.SMEM),
            pl.BlockSpec((1, lines, width), lambda g: (g, 0, 0)),
        ],
        out_specs=pl.BlockSpec((rows, columns, K), lambda g: (0, 0, 0)),
        compiler_params=pltpu.CompilerParams(vmem_limit_bytes=48 * 2**20),
        name="deposit",
    )(count, atoms)


def pull(count, atoms, potential):
    groups, lines, width = atoms.shape
    rows, columns, _ = potential.shape
    return pl.pallas_call(
        pull_kernel,
        out_shape=jax.ShapeDtypeStruct((groups, lines, width), jnp.float32),
        grid=(groups,),
        in_specs=[
            pl.BlockSpec(memory_space=pltpu.SMEM),
            pl.BlockSpec((1, lines, width), lambda g: (g, 0, 0)),
            pl.BlockSpec((rows, columns, K), lambda g: (0, 0, 0)),
        ],
        out_specs=pl.BlockSpec((1, lines, width), lambda g: (g, 0, 0)),
        scratch_shapes=[pltpu.VMEM((rows * columns, 3 * K), jnp.bfloat16)],
        compiler_params=pltpu.CompilerParams(vmem_limit_bytes=48 * 2**20),
        name="pull",
    )(count, atoms, potential)


def transformed(grid, span_x, span_y, rows_dev, cols_dev):
    matrix = jnp.asarray(hartley())
    packed = LANES // span_y
    bands = span_x // packed
    span_z = K // cols_dev
    slab = span_z // rows_dev
    identity = jnp.eye(packed, dtype=jnp.float32)
    mixing = (
        matrix.reshape(cols_dev, 1, span_y, 1, K) * identity[None, :, None, :, None]
    ).reshape(cols_dev, packed * span_y, packed * K)

    spectrum = lax.dot_general(matrix, grid, (((1,), (1,)), ((), ())), precision=HIGH)
    spectrum = spectrum.reshape(cols_dev, span_z, bands, LANES)
    spectrum = lax.all_to_all(spectrum, "py", split_axis=0, concat_axis=0, tiled=True)
    spectrum = jnp.einsum("szbl,slk->zbk", spectrum, mixing, precision=HIGH)
    spectrum = spectrum.reshape(rows_dev, slab, span_x, K)
    spectrum = lax.all_to_all(spectrum, "px", split_axis=0, concat_axis=0, tiled=True)
    split = matrix.reshape(K, rows_dev, span_x)
    spectrum = jnp.einsum("ksx,szxy->zky", split, spectrum, precision=HIGH)

    squared, profile = (jnp.asarray(table) for table in wave_profile())
    first = lax.axis_index("py") * span_z + lax.axis_index("px") * slab
    squared_z = lax.dynamic_slice(squared, (first,), (slab,))
    profile_z = lax.dynamic_slice(profile, (first,), (slab,))
    total = squared_z[:, None, None] + squared[None, :, None] + squared[None, None, :]
    gain = profile_z[:, None, None] * profile[None, :, None] * profile[None, None, :]
    kernel = jnp.where(
        total > 0, (EWALD_GAIN / float(K**3)) * gain / jnp.where(total > 0, total, 1.0), 0.0
    )
    spectrum = spectrum * kernel

    spectrum = jnp.einsum("ksx,zky->szxy", split, spectrum, precision=HIGH)
    spectrum = lax.all_to_all(spectrum, "px", split_axis=0, concat_axis=0, tiled=True)
    spectrum = spectrum.reshape(span_z, bands, packed * K)
    spectrum = jnp.einsum("zbk,slk->szbl", spectrum, mixing, precision=HIGH)
    spectrum = lax.all_to_all(spectrum, "py", split_axis=0, concat_axis=0, tiled=True)
    spectrum = spectrum.reshape(K, span_x * span_y)
    return lax.dot_general(spectrum, matrix, (((0,), (0,)), ((), ())), precision=HIGH)


def per_device(fractions, charge, cell_index, destination, live_blocks):
    rows_dev = lax.axis_size("px")
    cols_dev = lax.axis_size("py")
    span_x = K // rows_dev
    span_y = K // cols_dev
    blocks, width = charge.shape
    capacity = max(2, 3 * blocks // (2 * cols_dev))
    slots = cols_dev * capacity
    padded = -(-slots // GROUP_BLOCKS) * GROUP_BLOCKS
    groups = padded // GROUP_BLOCKS
    rows = -(-(span_x + 5) // ROWS_CHUNK) * ROWS_CHUNK
    columns = -(-(span_y + 5) // 8) * 8

    alive = (jnp.arange(blocks, dtype=jnp.int32) < live_blocks[0]).astype(jnp.int32)
    target = destination[:, 0]
    matches = (target[:, None] == jnp.arange(cols_dev, dtype=jnp.int32)[None, :]).astype(jnp.int32)
    matches = matches * alive[:, None]
    earlier = jnp.cumsum(matches, axis=0) - matches
    position = jnp.sum(earlier * matches, axis=1)
    slot_of = jnp.where(alive > 0, target * capacity + position, -1)
    picked = (slot_of[None, :] == jnp.arange(slots, dtype=jnp.int32)[:, None]).astype(jnp.float32)
    payload = jnp.stack(
        [
            fractions[:, 0],
            fractions[:, 1],
            fractions[:, 2],
            charge,
            (cell_index // (span_y * K)).astype(jnp.float32),
            (cell_index // K % span_y).astype(jnp.float32),
            (cell_index % K).astype(jnp.float32),
            jnp.ones(charge.shape, jnp.float32),
        ],
        axis=1,
    )
    outgoing = jnp.dot(picked, payload.reshape(blocks, -1), precision=HIGHEST)
    outgoing = outgoing.reshape(cols_dev, capacity, 8, width)
    arrived = lax.all_to_all(outgoing, "py", split_axis=0, concat_axis=0, tiled=True)
    arrived = arrived.reshape(slots, 8, width)
    used = (arrived[:, 7, 0] > 0.5).astype(jnp.int32)
    place = jnp.where(used > 0, jnp.cumsum(used) - used, -1)
    chosen = (place[None, :] == jnp.arange(padded, dtype=jnp.int32)[:, None]).astype(jnp.float32)
    atoms = jnp.dot(chosen, arrived.reshape(slots, -1), precision=HIGHEST)
    atoms = (
        atoms.reshape(groups, GROUP_BLOCKS, 8, width)
        .transpose(0, 2, 1, 3)
        .reshape(groups, 8, GROUP_BLOCKS * width)
    )
    count = ((jnp.sum(used) + GROUP_BLOCKS - 1) // GROUP_BLOCKS).reshape(1)

    extended = deposit(count, atoms, rows, columns)
    moved_rows = from_behind(extended[span_x : span_x + 5], "px", 1)
    extended = jnp.concatenate([extended[:5] + moved_rows, extended[5:span_x]], axis=0)
    moved_cols = from_behind(extended[:, span_y : span_y + 5], "py", 1)
    grid = jnp.concatenate([extended[:, :5] + moved_cols, extended[:, 5:span_y]], axis=1)

    potential = transformed(
        grid.reshape(span_x * span_y, K), span_x, span_y, rows_dev, cols_dev
    ).reshape(span_x, span_y, K)
    lower_rows = from_behind(potential[:5], "px", -1)
    potential = jnp.concatenate([potential, lower_rows], axis=0)
    lower_cols = from_behind(potential[:, :5], "py", -1)
    potential = jnp.concatenate([potential, lower_cols], axis=1)
    potential = jnp.pad(
        potential, ((0, rows - span_x - 5), (0, columns - span_y - 5), (0, 0))
    )

    forces = pull(count, atoms, potential)[:, :3]
    forces = (
        forces.reshape(groups, 3, GROUP_BLOCKS, width)
        .transpose(0, 2, 1, 3)
        .reshape(padded, 3 * width)
    )
    forces = lax.dot_general(chosen, forces, (((0,), (0,)), ((), ())), precision=HIGHEST)
    returned = lax.all_to_all(
        forces.reshape(cols_dev, capacity, 3, width), "py", split_axis=0, concat_axis=0, tiled=True
    ).reshape(slots, 3 * width)
    result = lax.dot_general(picked, returned, (((0,), (0,)), ((), ())), precision=HIGHEST)
    return result.reshape(blocks, 3, width)


def solution(mesh):
    split = (
        P(("px", "py"), None, None),
        P(("px", "py"), None),
        P(("px", "py"), None),
        P(("px", "py"), None),
        P(("px", "py")),
    )
    return jax.shard_map(
        per_device,
        mesh=mesh,
        in_specs=split,
        out_specs=P(("px", "py"), None, None),
        check_vma=False,
    )
```

```python
import math

import jax
import jax.numpy as jnp
import numpy as np
from jax import lax
from jax.experimental import pallas as pl
from jax.experimental.pallas import tpu as pltpu
from jax.sharding import PartitionSpec as P

K = 256
EWALD_GAIN = 4.0
EWALD_BETA = 0.6
SPLINE_SUMS = (1.0 / 120.0, 26.0 / 120.0, 66.0 / 120.0, 26.0 / 120.0, 1.0 / 120.0)
HIGHEST = lax.Precision.HIGHEST
HIGH = lax.Precision.HIGH
LANES = 128
ROWS_CHUNK = 14
GROUP_BLOCKS = 2


def hartley():
    steps = np.arange(K)
    angle = 2.0 * math.pi / K * (np.outer(steps, steps) % K)
    return (np.cos(angle) + np.sin(angle)).astype(np.float32)


def wave_profile():
    steps = np.arange(K)
    folded = np.where(2 * steps < K, steps, steps - K) / K
    waves = np.exp(2j * math.pi / K * np.outer(steps, np.arange(5)))
    modulus = 1.0 / np.abs(waves @ np.array(SPLINE_SUMS)) ** 2
    squared = folded * folded
    gauss = np.exp(-(math.pi * math.pi) * squared / (EWALD_BETA * EWALD_BETA))
    return squared.astype(np.float32), (gauss * modulus).astype(np.float32)


def from_behind(value, axis, steps):
    count = lax.axis_size(axis)
    pairs = [(source, (source + steps) % count) for source in range(count)]
    return lax.ppermute(value, axis, pairs)


def spline_six(u):
    older_values = [1.0 - u, u]
    slopes = []
    for spline_order in range(3, 7):
        newer_values = []
        for k in range(spline_order):
            terms = []
            if k >= 1:
                terms.append((u + (spline_order - 1 - k)) * older_values[k - 1])
            if k <= spline_order - 2:
                terms.append((k + 1 - u) * older_values[k])
            newer_values.append(sum(terms[1:], terms[0]) * (1.0 / (spline_order - 1)))
        if spline_order == 6:
            slopes = [-older_values[0]]
            slopes += [older_values[k - 1] - older_values[k] for k in range(1, 5)]
            slopes += [older_values[4]]
        older_values = newer_values
    return (older_values, slopes)


def placed(offset, values):
    table = jnp.zeros(offset.shape, jnp.float32)
    for k in range(6):
        table = jnp.where(offset == k, values[k], table)
    return table


def offsets(base, rows, wrap):
    width = base.shape[1]
    offset = lax.broadcasted_iota(jnp.int32, (rows, width), 0) - base
    return offset & (K - 1) if wrap else offset


def halves(value):
    upper = value.astype(jnp.bfloat16)
    lower = (value - upper.astype(jnp.float32)).astype(jnp.bfloat16)
    return upper, lower


def deposit_kernel(count_ref, atoms_ref, grid_ref):
    step = pl.program_id(0)
    rows, columns, depth = grid_ref.shape
    width = atoms_ref.shape[2]

    @pl.when(step == 0)
    def _():
        grid_ref[...] = jnp.zeros(grid_ref.shape, jnp.float32)

    @pl.when(step < count_ref[0])
    def _():
        atoms = atoms_ref[0]
        base = atoms.astype(jnp.int32)
        table_x = placed(offsets(base[4:5], rows, False), spline_six(atoms[0:1])[0])
        table_y = placed(offsets(base[5:6], columns, False), spline_six(atoms[1:2])[0])
        table_z = placed(offsets(base[6:7], depth, True), spline_six(atoms[2:3])[0])
        upper, lower = halves((table_z * atoms[3:4]).T)
        weights = jnp.concatenate([upper, lower, upper], axis=0)
        for start in range(0, rows, ROWS_CHUNK):
            chunk = table_x[start : start + ROWS_CHUNK]
            outer = (chunk[:, None, :] * table_y[None, :, :]).reshape(-1, width)
            upper, lower = halves(outer)
            spread = jnp.dot(
                jnp.concatenate([upper, upper, lower], axis=1),
                weights,
                preferred_element_type=jnp.float32,
            )
            grid_ref[start : start + ROWS_CHUNK] += spread.reshape(-1, columns, depth)


def pull_kernel(count_ref, atoms_ref, potential_ref, forces_ref, parts):
    step = pl.program_id(0)
    rows, columns, depth = potential_ref.shape
    width = atoms_ref.shape[2]
    piece = ROWS_CHUNK * columns

    @pl.when(step == 0)
    def _():
        for index in range(rows // ROWS_CHUNK):
            start = index * ROWS_CHUNK
            values = potential_ref[start : start + ROWS_CHUNK].reshape(piece, depth)
            upper, lower = halves(values)
            parts[index * piece : (index + 1) * piece] = jnp.concatenate(
                [upper, lower, upper], axis=1
            )

    @pl.when(step >= count_ref[0])
    def _():
        forces_ref[...] = jnp.zeros(forces_ref.shape, jnp.float32)

    @pl.when(step < count_ref[0])
    def _():
        atoms = atoms_ref[0]
        base = atoms.astype(jnp.int32)
        offset_x = offsets(base[4:5], rows, False)
        offset_y = offsets(base[5:6], columns, False)
        offset_z = offsets(base[6:7], depth, True)
        values, slopes = spline_six(atoms[0:1])
        table_x, slope_x = placed(offset_x, values), placed(offset_x, slopes)
        values, slopes = spline_six(atoms[1:2])
        table_y, slope_y = placed(offset_y, values), placed(offset_y, slopes)
        values, slopes = spline_six(atoms[2:3])
        both = jnp.concatenate([placed(offset_z, values), placed(offset_z, slopes)], axis=1)
        upper, lower = halves(both)
        weights = jnp.concatenate([upper, upper, lower], axis=0)
        totals = [jnp.zeros((8, width), jnp.float32) for _ in range(3)]
        for index in range(rows // ROWS_CHUNK):
            start = index * ROWS_CHUNK
            sampled = jnp.dot(
                parts[index * piece : (index + 1) * piece],
                weights,
                preferred_element_type=jnp.float32,
            ).reshape(ROWS_CHUNK, columns, 2 * width)
            for row in range(ROWS_CHUNK):
                plain = sampled[row, :, :width]
                sloped = sampled[row, :, width:]
                value_x = table_x[start + row : start + row + 1]
                turned_x = slope_x[start + row : start + row + 1]

                def folded(terms):
                    return jnp.sum(terms.reshape(columns // 8, 8, width), axis=0)

                totals[0] = totals[0] + turned_x * folded(plain * table_y)
                totals[1] = totals[1] + value_x * folded(plain * slope_y)
                totals[2] = totals[2] + value_x * folded(sloped * table_y)
        result = [-atoms[3:4] * jnp.sum(total, axis=0, keepdims=True) for total in totals]
        forces_ref[0] = jnp.concatenate(
            result + [jnp.zeros((5, width), jnp.float32)], axis=0
        )


def deposit(count, atoms, rows, columns):
    groups, lines, width = atoms.shape
    return pl.pallas_call(
        deposit_kernel,
        out_shape=jax.ShapeDtypeStruct((rows, columns, K), jnp.float32),
        grid=(groups,),
        in_specs=[
            pl.BlockSpec(memory_space=pltpu.SMEM),
            pl.BlockSpec((1, lines, width), lambda g: (g, 0, 0)),
        ],
        out_specs=pl.BlockSpec((rows, columns, K), lambda g: (0, 0, 0)),
        compiler_params=pltpu.CompilerParams(vmem_limit_bytes=48 * 2**20),
        name="deposit",
    )(count, atoms)


def pull(count, atoms, potential):
    groups, lines, width = atoms.shape
    rows, columns, _ = potential.shape
    return pl.pallas_call(
        pull_kernel,
        out_shape=jax.ShapeDtypeStruct((groups, lines, width), jnp.float32),
        grid=(groups,),
        in_specs=[
            pl.BlockSpec(memory_space=pltpu.SMEM),
            pl.BlockSpec((1, lines, width), lambda g: (g, 0, 0)),
            pl.BlockSpec((rows, columns, K), lambda g: (0, 0, 0)),
        ],
        out_specs=pl.BlockSpec((1, lines, width), lambda g: (g, 0, 0)),
        scratch_shapes=[pltpu.VMEM((rows * columns, 3 * K), jnp.bfloat16)],
        compiler_params=pltpu.CompilerParams(vmem_limit_bytes=48 * 2**20),
        name="pull",
    )(count, atoms, potential)


def exact_halves(values):
    upper = values.astype(jnp.bfloat16)
    return upper, (values - upper.astype(np.float32)).astype(jnp.bfloat16)


def product(left, right, transposed=False):
    dims = (((1,), (1 if transposed else 0,)), ((), ()))

    def one(a, b):
        return lax.dot_general(a, b, dims, preferred_element_type=jnp.float32)

    return one(left[0], right[0]) + (one(left[1], right[0]) + one(left[0], right[1]))


def convolve_kernel(
    counts,
    spectrum_ref,
    gain_ref,
    mix_upper,
    mix_lower,
    wave_upper,
    wave_lower,
    out_ref,
    columns_in,
    rows_out,
    rows_in,
    back_out,
    back_in,
    columns_out,
    send_sems,
    recv_sems,
    local_sems,
):
    chunks, step, bands = counts
    rows_dev = lax.axis_size("px")
    cols_dev = lax.axis_size("py")
    index_x = lax.axis_index("px")
    index_y = lax.axis_index("py")
    lines = step * bands
    packed = mix_upper.shape[1] // K
    span_x = packed * bands

    barrier = pltpu.get_barrier_semaphore()
    for axis, count, index in (("px", rows_dev, index_x), ("py", cols_dev, index_y)):
        for shift in range(1, count):
            pl.semaphore_signal(
                barrier,
                inc=1,
                device_id={axis: lax.rem(index + shift, count)},
                device_id_type=pl.DeviceIdType.MESH,
            )
    pl.semaphore_wait(barrier, rows_dev + cols_dev - 2)

    def exchange(stage, chunk, axis, source, target):
        count, index = (rows_dev, index_x) if axis == "px" else (cols_dev, index_y)
        copies = []
        for shift in range(1, count):
            peer = lax.rem(index + shift, count)
            copies.append(
                pltpu.make_async_remote_copy(
                    src_ref=source(peer),
                    dst_ref=target(index),
                    send_sem=send_sems.at[stage, chunk, shift],
                    recv_sem=recv_sems.at[stage, chunk, shift],
                    device_id={axis: peer},
                    device_id_type=pl.DeviceIdType.MESH,
                )
            )
        copies.append(
            pltpu.make_async_copy(source(index), target(index), local_sems.at[stage, chunk])
        )
        for copy in copies:
            copy.start()
        return copies

    def arrived(copies):
        for copy in copies[:-1]:
            copy.wait_recv()
        copies[-1].wait()

    def lanes(index):
        return pl.ds(pl.multiple_of(index * LANES, LANES), LANES)

    def band_rows(index):
        return pl.ds(pl.multiple_of(index * span_x, span_x), span_x)

    started = []
    first, second, third, fourth = [], [], [], []
    for h in range(chunks):
        part = pl.ds(h * lines, lines)
        first.append(
            exchange(
                0,
                h,
                "py",
                lambda peer: spectrum_ref.at[peer, :, part],
                lambda index: columns_in.at[h, :, :, lanes(index)],
            )
        )
    for h in range(chunks):
        arrived(first[h])
        values = columns_in[h].reshape(rows_dev * lines, cols_dev * LANES)
        mixed = product(halves(values), (mix_upper[...], mix_lower[...]))
        for r in range(rows_dev):
            for j in range(step):
                start = r * lines + j * bands
                for p in range(packed):
                    rows_out[h, r, j, p * bands : (p + 1) * bands, :] = mixed[
                        start : start + bands, p * K : (p + 1) * K
                    ]
        second.append(
            exchange(
                1,
                h,
                "px",
                lambda peer: rows_out.at[h, peer],
                lambda index: rows_in.at[h, :, band_rows(index)],
            )
        )
    for h in range(chunks):
        arrived(second[h])
        wave = (wave_upper[...], wave_lower[...])
        for j in range(step):
            mixed = product(wave, halves(rows_in[h, j])) * gain_ref[h * step + j]
            back_out[h, j] = product(wave, halves(mixed))
        third.append(
            exchange(
                2,
                h,
                "px",
                lambda peer: back_out.at[h, :, band_rows(peer)],
                lambda index: back_in.at[h, index],
            )
        )
    for h in range(chunks):
        arrived(third[h])
        values = jnp.concatenate(
            [
                jnp.concatenate(
                    [back_in[h, r, j, p * bands : (p + 1) * bands, :] for p in range(packed)],
                    axis=1,
                )
                for r in range(rows_dev)
                for j in range(step)
            ],
            axis=0,
        )
        mixed = product(halves(values), (mix_upper[...], mix_lower[...]), transposed=True)
        columns_out[h] = mixed.reshape(rows_dev, lines, cols_dev * LANES)
        part = pl.ds(h * lines, lines)
        fourth.append(
            exchange(
                3,
                h,
                "py",
                lambda peer: columns_out.at[h, :, :, lanes(peer)],
                lambda index: out_ref.at[index, :, part],
            )
        )
    for h in range(chunks):
        arrived(fourth[h])
    for stage in (first, second, third, fourth):
        for copies in stage:
            for copy in copies[:-1]:
                copy.wait_send()


def convolve(spectrum, gain, mixing, matrix, bands):
    cols_dev, rows_dev, held, _ = spectrum.shape
    slab = held // bands
    chunks = 4
    while slab % chunks or (slab // chunks * bands) % 8:
        chunks //= 2
    step = slab // chunks
    lines = step * bands
    span_x = K // rows_dev
    peers = max(rows_dev, cols_dev)
    mix_upper, mix_lower = exact_halves(mixing)
    wave_upper, wave_lower = exact_halves(matrix)
    columns_shape = (chunks, rows_dev, lines, cols_dev * LANES)
    rows_shape = (chunks, rows_dev, step, span_x, K)
    full_shape = (chunks, step, K, K)

    def body(*refs):
        convolve_kernel((chunks, step, bands), *refs)

    whole = pl.BlockSpec(memory_space=pltpu.VMEM)
    return pl.pallas_call(
        body,
        out_shape=jax.ShapeDtypeStruct(spectrum.shape, jnp.float32),
        in_specs=[whole] * 6,
        out_specs=whole,
        scratch_shapes=[
            pltpu.VMEM(columns_shape, jnp.float32),
            pltpu.VMEM(rows_shape, jnp.float32),
            pltpu.VMEM(full_shape, jnp.float32),
            pltpu.VMEM(full_shape, jnp.float32),
            pltpu.VMEM(rows_shape, jnp.float32),
            pltpu.VMEM(columns_shape, jnp.float32),
            pltpu.SemaphoreType.DMA((4, chunks, peers)),
            pltpu.SemaphoreType.DMA((4, chunks, peers)),
            pltpu.SemaphoreType.DMA((4, chunks)),
        ],
        compiler_params=pltpu.CompilerParams(
            collective_id=0, has_side_effects=True, vmem_limit_bytes=56 * 2**20
        ),
        name="convolve",
    )(
        spectrum,
        gain,
        jnp.asarray(mix_upper),
        jnp.asarray(mix_lower),
        jnp.asarray(wave_upper),
        jnp.asarray(wave_lower),
    )


def transformed(grid, span_x, span_y, rows_dev, cols_dev):
    table = hartley()
    matrix = jnp.asarray(table)
    packed = LANES // span_y
    bands = span_x // packed
    span_z = K // cols_dev
    slab = span_z // rows_dev
    mixing = np.einsum("syk,pq->spyqk", table.reshape(cols_dev, span_y, K), np.eye(packed))
    mixing = mixing.reshape(cols_dev * LANES, packed * K).astype(np.float32)

    squared, profile = (jnp.asarray(values) for values in wave_profile())
    first = lax.axis_index("py") * span_z + lax.axis_index("px") * slab
    squared_z = lax.dynamic_slice(squared, (first,), (slab,))
    profile_z = lax.dynamic_slice(profile, (first,), (slab,))
    total = squared_z[:, None, None] + squared[None, :, None] + squared[None, None, :]
    gain = profile_z[:, None, None] * profile[None, :, None] * profile[None, None, :]
    gain = jnp.where(
        total > 0, (EWALD_GAIN / float(K**3)) * gain / jnp.where(total > 0, total, 1.0), 0.0
    )

    ordered = grid.reshape(packed, bands, span_y, K).transpose(1, 0, 2, 3).reshape(-1, K)
    spectrum = lax.dot_general(matrix, ordered, (((1,), (1,)), ((), ())), precision=HIGH)
    spectrum = spectrum.reshape(cols_dev, rows_dev, slab * bands, LANES)
    spectrum = convolve(spectrum, gain, mixing, table, bands)
    spectrum = spectrum.reshape(K, span_x * span_y)
    ordered = lax.dot_general(spectrum, matrix, (((0,), (0,)), ((), ())), precision=HIGH)
    return ordered.reshape(bands, packed, span_y, K).transpose(1, 0, 2, 3)


def per_device(fractions, charge, cell_index, destination, live_blocks):
    rows_dev = lax.axis_size("px")
    cols_dev = lax.axis_size("py")
    span_x = K // rows_dev
    span_y = K // cols_dev
    blocks, width = charge.shape
    capacity = max(2, 3 * blocks // (2 * cols_dev))
    slots = cols_dev * capacity
    padded = -(-slots // GROUP_BLOCKS) * GROUP_BLOCKS
    groups = padded // GROUP_BLOCKS
    rows = -(-(span_x + 5) // ROWS_CHUNK) * ROWS_CHUNK
    columns = -(-(span_y + 5) // 8) * 8

    alive = (jnp.arange(blocks, dtype=jnp.int32) < live_blocks[0]).astype(jnp.int32)
    target = destination[:, 0]
    matches = (target[:, None] == jnp.arange(cols_dev, dtype=jnp.int32)[None, :]).astype(jnp.int32)
    matches = matches * alive[:, None]
    earlier = jnp.cumsum(matches, axis=0) - matches
    position = jnp.sum(earlier * matches, axis=1)
    slot_of = jnp.where(alive > 0, target * capacity + position, -1)
    picked = (slot_of[None, :] == jnp.arange(slots, dtype=jnp.int32)[:, None]).astype(jnp.float32)
    payload = jnp.stack(
        [
            fractions[:, 0],
            fractions[:, 1],
            fractions[:, 2],
            charge,
            (cell_index // (span_y * K)).astype(jnp.float32),
            (cell_index // K % span_y).astype(jnp.float32),
            (cell_index % K).astype(jnp.float32),
            jnp.ones(charge.shape, jnp.float32),
        ],
        axis=1,
    )
    outgoing = jnp.dot(picked, payload.reshape(blocks, -1), precision=HIGHEST)
    outgoing = outgoing.reshape(cols_dev, capacity, 8, width)
    arrived = lax.all_to_all(outgoing, "py", split_axis=0, concat_axis=0, tiled=True)
    arrived = arrived.reshape(slots, 8, width)
    used = (arrived[:, 7, 0] > 0.5).astype(jnp.int32)
    place = jnp.where(used > 0, jnp.cumsum(used) - used, -1)
    chosen = (place[None, :] == jnp.arange(padded, dtype=jnp.int32)[:, None]).astype(jnp.float32)
    atoms = jnp.dot(chosen, arrived.reshape(slots, -1), precision=HIGHEST)
    atoms = (
        atoms.reshape(groups, GROUP_BLOCKS, 8, width)
        .transpose(0, 2, 1, 3)
        .reshape(groups, 8, GROUP_BLOCKS * width)
    )
    count = ((jnp.sum(used) + GROUP_BLOCKS - 1) // GROUP_BLOCKS).reshape(1)

    extended = deposit(count, atoms, rows, columns)
    moved_rows = from_behind(extended[span_x : span_x + 5], "px", 1)
    extended = jnp.concatenate([extended[:5] + moved_rows, extended[5:span_x]], axis=0)
    moved_cols = from_behind(extended[:, span_y : span_y + 5], "py", 1)
    grid = jnp.concatenate([extended[:, :5] + moved_cols, extended[:, 5:span_y]], axis=1)

    potential = transformed(
        grid.reshape(span_x * span_y, K), span_x, span_y, rows_dev, cols_dev
    ).reshape(span_x, span_y, K)
    lower_rows = from_behind(potential[:5], "px", -1)
    potential = jnp.concatenate([potential, lower_rows], axis=0)
    lower_cols = from_behind(potential[:, :5], "py", -1)
    potential = jnp.concatenate([potential, lower_cols], axis=1)
    potential = jnp.pad(
        potential, ((0, rows - span_x - 5), (0, columns - span_y - 5), (0, 0))
    )

    forces = pull(count, atoms, potential)[:, :3]
    forces = (
        forces.reshape(groups, 3, GROUP_BLOCKS, width)
        .transpose(0, 2, 1, 3)
        .reshape(padded, 3 * width)
    )
    forces = lax.dot_general(chosen, forces, (((0,), (0,)), ((), ())), precision=HIGHEST)
    returned = lax.all_to_all(
        forces.reshape(cols_dev, capacity, 3, width), "py", split_axis=0, concat_axis=0, tiled=True
    ).reshape(slots, 3 * width)
    result = lax.dot_general(picked, returned, (((0,), (0,)), ((), ())), precision=HIGHEST)
    return result.reshape(blocks, 3, width)


def solution(mesh):
    split = (
        P(("px", "py"), None, None),
        P(("px", "py"), None),
        P(("px", "py"), None),
        P(("px", "py"), None),
        P(("px", "py")),
    )
    return jax.shard_map(
        per_device,
        mesh=mesh,
        in_specs=split,
        out_specs=P(("px", "py"), None, None),
        check_vma=False,
    )
```

```python
import math

import jax
import jax.numpy as jnp
import numpy as np
from jax import lax
from jax.experimental import pallas as pl
from jax.experimental.pallas import tpu as pltpu
from jax.sharding import PartitionSpec as P

K = 256
EWALD_GAIN = 4.0
EWALD_BETA = 0.6
SPLINE_SUMS = (1.0 / 120.0, 26.0 / 120.0, 66.0 / 120.0, 26.0 / 120.0, 1.0 / 120.0)
HIGHEST = lax.Precision.HIGHEST
HIGH = lax.Precision.HIGH
LANES = 128
ROWS_CHUNK = 10
SORT_BLOCKS = 8
GROUP_BLOCKS = 2


def hartley():
    steps = np.arange(K)
    angle = 2.0 * math.pi / K * (np.outer(steps, steps) % K)
    return (np.cos(angle) + np.sin(angle)).astype(np.float32)


def wave_profile():
    steps = np.arange(K)
    folded = np.where(2 * steps < K, steps, steps - K) / K
    waves = np.exp(2j * math.pi / K * np.outer(steps, np.arange(5)))
    modulus = 1.0 / np.abs(waves @ np.array(SPLINE_SUMS)) ** 2
    squared = folded * folded
    gauss = np.exp(-(math.pi * math.pi) * squared / (EWALD_BETA * EWALD_BETA))
    return squared.astype(np.float32), (gauss * modulus).astype(np.float32)


def from_behind(value, axis, steps):
    count = lax.axis_size(axis)
    pairs = [(source, (source + steps) % count) for source in range(count)]
    return lax.ppermute(value, axis, pairs)


def spline_six(u):
    older_values = [1.0 - u, u]
    slopes = []
    for spline_order in range(3, 7):
        newer_values = []
        for k in range(spline_order):
            terms = []
            if k >= 1:
                terms.append((u + (spline_order - 1 - k)) * older_values[k - 1])
            if k <= spline_order - 2:
                terms.append((k + 1 - u) * older_values[k])
            newer_values.append(sum(terms[1:], terms[0]) * (1.0 / (spline_order - 1)))
        if spline_order == 6:
            slopes = [-older_values[0]]
            slopes += [older_values[k - 1] - older_values[k] for k in range(1, 5)]
            slopes += [older_values[4]]
        older_values = newer_values
    return (older_values, slopes)


def placed(offset, values):
    table = jnp.zeros(offset.shape, jnp.float32)
    for k in range(6):
        table = jnp.where(offset == k, values[k], table)
    return table


def offsets(base, rows, wrap):
    width = base.shape[1]
    offset = lax.broadcasted_iota(jnp.int32, (rows, width), 0) - base
    return offset & (K - 1) if wrap else offset


def halves(value):
    upper = value.astype(jnp.bfloat16)
    lower = (value - upper.astype(jnp.float32)).astype(jnp.bfloat16)
    return upper, lower


def touched(span_ref, step, start):
    return (span_ref[0, step] < start + ROWS_CHUNK) & (span_ref[1, step] + 5 >= start)


def deposit_kernel(span_ref, atoms_ref, grid_ref):
    step = pl.program_id(0)
    rows, columns, depth = grid_ref.shape
    width = atoms_ref.shape[2]

    @pl.when(step == 0)
    def _():
        grid_ref[...] = jnp.zeros(grid_ref.shape, jnp.float32)

    @pl.when(span_ref[1, step] >= 0)
    def _():
        atoms = atoms_ref[0]
        base = atoms.astype(jnp.int32)
        table_x = placed(offsets(base[4:5], rows, False), spline_six(atoms[0:1])[0])
        table_y = placed(offsets(base[5:6], columns, False), spline_six(atoms[1:2])[0])
        table_z = placed(offsets(base[6:7], depth, True), spline_six(atoms[2:3])[0])
        upper, lower = halves((table_z * atoms[3:4]).T)
        weights = jnp.concatenate([upper, lower, upper], axis=0)
        for start in range(0, rows, ROWS_CHUNK):

            @pl.when(touched(span_ref, step, start))
            def _(start=start):
                chunk = table_x[start : start + ROWS_CHUNK]
                outer = (chunk[:, None, :] * table_y[None, :, :]).reshape(-1, width)
                upper, lower = halves(outer)
                spread = jnp.dot(
                    jnp.concatenate([upper, upper, lower], axis=1),
                    weights,
                    preferred_element_type=jnp.float32,
                )
                grid_ref[start : start + ROWS_CHUNK] += spread.reshape(-1, columns, depth)


def pull_kernel(span_ref, atoms_ref, potential_ref, forces_ref, parts, totals):
    step = pl.program_id(0)
    rows, columns, depth = potential_ref.shape
    width = atoms_ref.shape[2]
    piece = ROWS_CHUNK * columns

    @pl.when(step == 0)
    def _():
        for index in range(rows // ROWS_CHUNK):
            start = index * ROWS_CHUNK
            values = potential_ref[start : start + ROWS_CHUNK].reshape(piece, depth)
            upper, lower = halves(values)
            parts[index * piece : (index + 1) * piece] = jnp.concatenate(
                [upper, lower, upper], axis=1
            )

    @pl.when(span_ref[1, step] < 0)
    def _():
        forces_ref[...] = jnp.zeros(forces_ref.shape, jnp.float32)

    @pl.when(span_ref[1, step] >= 0)
    def _():
        atoms = atoms_ref[0]
        base = atoms.astype(jnp.int32)
        offset_x = offsets(base[4:5], rows, False)
        offset_y = offsets(base[5:6], columns, False)
        offset_z = offsets(base[6:7], depth, True)
        values, slopes = spline_six(atoms[0:1])
        table_x, slope_x = placed(offset_x, values), placed(offset_x, slopes)
        values, slopes = spline_six(atoms[1:2])
        table_y, slope_y = placed(offset_y, values), placed(offset_y, slopes)
        values, slopes = spline_six(atoms[2:3])
        both = jnp.concatenate([placed(offset_z, values), placed(offset_z, slopes)], axis=1)
        upper, lower = halves(both)
        weights = jnp.concatenate([upper, upper, lower], axis=0)
        totals[...] = jnp.zeros(totals.shape, jnp.float32)

        def folded(terms):
            return jnp.sum(terms.reshape(columns // 8, 8, width), axis=0)

        for index in range(rows // ROWS_CHUNK):

            @pl.when(touched(span_ref, step, index * ROWS_CHUNK))
            def _(index=index):
                start = index * ROWS_CHUNK
                sampled = jnp.dot(
                    parts[index * piece : (index + 1) * piece],
                    weights,
                    preferred_element_type=jnp.float32,
                ).reshape(ROWS_CHUNK, columns, 2 * width)
                sums = [totals[0], totals[1], totals[2]]
                for row in range(ROWS_CHUNK):
                    plain = sampled[row, :, :width]
                    sloped = sampled[row, :, width:]
                    value_x = table_x[start + row : start + row + 1]
                    turned_x = slope_x[start + row : start + row + 1]
                    sums[0] = sums[0] + turned_x * folded(plain * table_y)
                    sums[1] = sums[1] + value_x * folded(plain * slope_y)
                    sums[2] = sums[2] + value_x * folded(sloped * table_y)
                for axis in range(3):
                    totals[axis] = sums[axis]

        result = [-atoms[3:4] * jnp.sum(totals[axis], axis=0, keepdims=True) for axis in range(3)]
        forces_ref[0] = jnp.concatenate(
            result + [jnp.zeros((5, width), jnp.float32)], axis=0
        )


def deposit(count, atoms, rows, columns):
    groups, lines, width = atoms.shape
    return pl.pallas_call(
        deposit_kernel,
        out_shape=jax.ShapeDtypeStruct((rows, columns, K), jnp.float32),
        grid=(groups,),
        in_specs=[
            pl.BlockSpec(memory_space=pltpu.SMEM),
            pl.BlockSpec((1, lines, width), lambda g: (g, 0, 0)),
        ],
        out_specs=pl.BlockSpec((rows, columns, K), lambda g: (0, 0, 0)),
        compiler_params=pltpu.CompilerParams(vmem_limit_bytes=48 * 2**20),
        name="deposit",
    )(count, atoms)


def pull(count, atoms, potential):
    groups, lines, width = atoms.shape
    rows, columns, _ = potential.shape
    return pl.pallas_call(
        pull_kernel,
        out_shape=jax.ShapeDtypeStruct((groups, lines, width), jnp.float32),
        grid=(groups,),
        in_specs=[
            pl.BlockSpec(memory_space=pltpu.SMEM),
            pl.BlockSpec((1, lines, width), lambda g: (g, 0, 0)),
            pl.BlockSpec((rows, columns, K), lambda g: (0, 0, 0)),
        ],
        out_specs=pl.BlockSpec((1, lines, width), lambda g: (g, 0, 0)),
        scratch_shapes=[
            pltpu.VMEM((rows * columns, 3 * K), jnp.bfloat16),
            pltpu.VMEM((3, 8, width), jnp.float32),
        ],
        compiler_params=pltpu.CompilerParams(vmem_limit_bytes=48 * 2**20),
        name="pull",
    )(count, atoms, potential)


def exact_halves(values):
    upper = values.astype(jnp.bfloat16)
    return upper, (values - upper.astype(np.float32)).astype(jnp.bfloat16)


def product(left, right, transposed=False):
    dims = (((1,), (1 if transposed else 0,)), ((), ()))

    def one(a, b):
        return lax.dot_general(a, b, dims, preferred_element_type=jnp.float32)

    return one(left[0], right[0]) + (one(left[1], right[0]) + one(left[0], right[1]))


def convolve_kernel(
    counts,
    spectrum_ref,
    gain_ref,
    mix_upper,
    mix_lower,
    wave_upper,
    wave_lower,
    out_ref,
    columns_in,
    rows_out,
    rows_in,
    back_out,
    back_in,
    columns_out,
    send_sems,
    recv_sems,
    local_sems,
):
    chunks, step, bands = counts
    rows_dev = lax.axis_size("px")
    cols_dev = lax.axis_size("py")
    index_x = lax.axis_index("px")
    index_y = lax.axis_index("py")
    lines = step * bands
    packed = mix_upper.shape[1] // K
    span_x = packed * bands

    barrier = pltpu.get_barrier_semaphore()
    for axis, count, index in (("px", rows_dev, index_x), ("py", cols_dev, index_y)):
        for shift in range(1, count):
            pl.semaphore_signal(
                barrier,
                inc=1,
                device_id={axis: lax.rem(index + shift, count)},
                device_id_type=pl.DeviceIdType.MESH,
            )
    pl.semaphore_wait(barrier, rows_dev + cols_dev - 2)

    def exchange(stage, chunk, axis, source, target):
        count, index = (rows_dev, index_x) if axis == "px" else (cols_dev, index_y)
        copies = []
        for shift in range(1, count):
            peer = lax.rem(index + shift, count)
            copies.append(
                pltpu.make_async_remote_copy(
                    src_ref=source(peer),
                    dst_ref=target(index),
                    send_sem=send_sems.at[stage, chunk, shift],
                    recv_sem=recv_sems.at[stage, chunk, shift],
                    device_id={axis: peer},
                    device_id_type=pl.DeviceIdType.MESH,
                )
            )
        copies.append(
            pltpu.make_async_copy(source(index), target(index), local_sems.at[stage, chunk])
        )
        for copy in copies:
            copy.start()
        return copies

    def arrived(copies):
        for copy in copies[:-1]:
            copy.wait_recv()
        copies[-1].wait()

    def lanes(index):
        return pl.ds(pl.multiple_of(index * LANES, LANES), LANES)

    def band_rows(index):
        return pl.ds(pl.multiple_of(index * span_x, span_x), span_x)

    started = []
    first, second, third, fourth = [], [], [], []
    for h in range(chunks):
        part = pl.ds(h * lines, lines)
        first.append(
            exchange(
                0,
                h,
                "py",
                lambda peer: spectrum_ref.at[peer, :, part],
                lambda index: columns_in.at[h, :, :, lanes(index)],
            )
        )
    for h in range(chunks):
        arrived(first[h])
        values = columns_in[h].reshape(rows_dev * lines, cols_dev * LANES)
        mixed = product(halves(values), (mix_upper[...], mix_lower[...]))
        for r in range(rows_dev):
            for j in range(step):
                start = r * lines + j * bands
                for p in range(packed):
                    rows_out[h, r, j, p * bands : (p + 1) * bands, :] = mixed[
                        start : start + bands, p * K : (p + 1) * K
                    ]
        second.append(
            exchange(
                1,
                h,
                "px",
                lambda peer: rows_out.at[h, peer],
                lambda index: rows_in.at[h, :, band_rows(index)],
            )
        )
    for h in range(chunks):
        arrived(second[h])
        wave = (wave_upper[...], wave_lower[...])
        for j in range(step):
            mixed = product(wave, halves(rows_in[h, j])) * gain_ref[h * step + j]
            back_out[h, j] = product(wave, halves(mixed))
        third.append(
            exchange(
                2,
                h,
                "px",
                lambda peer: back_out.at[h, :, band_rows(peer)],
                lambda index: back_in.at[h, index],
            )
        )
    for h in range(chunks):
        arrived(third[h])
        values = jnp.concatenate(
            [
                jnp.concatenate(
                    [back_in[h, r, j, p * bands : (p + 1) * bands, :] for p in range(packed)],
                    axis=1,
                )
                for r in range(rows_dev)
                for j in range(step)
            ],
            axis=0,
        )
        mixed = product(halves(values), (mix_upper[...], mix_lower[...]), transposed=True)
        columns_out[h] = mixed.reshape(rows_dev, lines, cols_dev * LANES)
        part = pl.ds(h * lines, lines)
        fourth.append(
            exchange(
                3,
                h,
                "py",
                lambda peer: columns_out.at[h, :, :, lanes(peer)],
                lambda index: out_ref.at[index, :, part],
            )
        )
    for h in range(chunks):
        arrived(fourth[h])
    for stage in (first, second, third, fourth):
        for copies in stage:
            for copy in copies[:-1]:
                copy.wait_send()


def convolve(spectrum, gain, mixing, matrix, bands):
    cols_dev, rows_dev, held, _ = spectrum.shape
    slab = held // bands
    chunks = 4
    while slab % chunks or (slab // chunks * bands) % 8:
        chunks //= 2
    step = slab // chunks
    lines = step * bands
    span_x = K // rows_dev
    peers = max(rows_dev, cols_dev)
    mix_upper, mix_lower = exact_halves(mixing)
    wave_upper, wave_lower = exact_halves(matrix)
    columns_shape = (chunks, rows_dev, lines, cols_dev * LANES)
    rows_shape = (chunks, rows_dev, step, span_x, K)
    full_shape = (chunks, step, K, K)

    def body(*refs):
        convolve_kernel((chunks, step, bands), *refs)

    whole = pl.BlockSpec(memory_space=pltpu.VMEM)
    return pl.pallas_call(
        body,
        out_shape=jax.ShapeDtypeStruct(spectrum.shape, jnp.float32),
        in_specs=[whole] * 6,
        out_specs=whole,
        scratch_shapes=[
            pltpu.VMEM(columns_shape, jnp.float32),
            pltpu.VMEM(rows_shape, jnp.float32),
            pltpu.VMEM(full_shape, jnp.float32),
            pltpu.VMEM(full_shape, jnp.float32),
            pltpu.VMEM(rows_shape, jnp.float32),
            pltpu.VMEM(columns_shape, jnp.float32),
            pltpu.SemaphoreType.DMA((4, chunks, peers)),
            pltpu.SemaphoreType.DMA((4, chunks, peers)),
            pltpu.SemaphoreType.DMA((4, chunks)),
        ],
        compiler_params=pltpu.CompilerParams(
            collective_id=0, has_side_effects=True, vmem_limit_bytes=56 * 2**20
        ),
        name="convolve",
    )(
        spectrum,
        gain,
        jnp.asarray(mix_upper),
        jnp.asarray(mix_lower),
        jnp.asarray(wave_upper),
        jnp.asarray(wave_lower),
    )


def transformed(grid, span_x, span_y, rows_dev, cols_dev):
    table = hartley()
    matrix = jnp.asarray(table)
    packed = LANES // span_y
    bands = span_x // packed
    span_z = K // cols_dev
    slab = span_z // rows_dev
    mixing = np.einsum("syk,pq->spyqk", table.reshape(cols_dev, span_y, K), np.eye(packed))
    mixing = mixing.reshape(cols_dev * LANES, packed * K).astype(np.float32)

    squared, profile = (jnp.asarray(values) for values in wave_profile())
    first = lax.axis_index("py") * span_z + lax.axis_index("px") * slab
    squared_z = lax.dynamic_slice(squared, (first,), (slab,))
    profile_z = lax.dynamic_slice(profile, (first,), (slab,))
    total = squared_z[:, None, None] + squared[None, :, None] + squared[None, None, :]
    gain = profile_z[:, None, None] * profile[None, :, None] * profile[None, None, :]
    gain = jnp.where(
        total > 0, (EWALD_GAIN / float(K**3)) * gain / jnp.where(total > 0, total, 1.0), 0.0
    )

    ordered = grid.reshape(packed, bands, span_y, K).transpose(1, 0, 2, 3).reshape(-1, K)
    spectrum = lax.dot_general(matrix, ordered, (((1,), (1,)), ((), ())), precision=HIGH)
    spectrum = spectrum.reshape(cols_dev, rows_dev, slab * bands, LANES)
    spectrum = convolve(spectrum, gain, mixing, table, bands)
    spectrum = spectrum.reshape(K, span_x * span_y)
    ordered = lax.dot_general(spectrum, matrix, (((0,), (0,)), ((), ())), precision=HIGH)
    return ordered.reshape(bands, packed, span_y, K).transpose(1, 0, 2, 3)


def per_device(fractions, charge, cell_index, destination, live_blocks):
    rows_dev = lax.axis_size("px")
    cols_dev = lax.axis_size("py")
    span_x = K // rows_dev
    span_y = K // cols_dev
    blocks, width = charge.shape
    capacity = max(2, 3 * blocks // (2 * cols_dev))
    slots = cols_dev * capacity
    padded = -(-slots // SORT_BLOCKS) * SORT_BLOCKS
    groups = padded // GROUP_BLOCKS
    rows = -(-(span_x + 5) // ROWS_CHUNK) * ROWS_CHUNK
    columns = -(-(span_y + 5) // 8) * 8

    alive = (jnp.arange(blocks, dtype=jnp.int32) < live_blocks[0]).astype(jnp.int32)
    target = destination[:, 0]
    matches = (target[:, None] == jnp.arange(cols_dev, dtype=jnp.int32)[None, :]).astype(jnp.int32)
    matches = matches * alive[:, None]
    earlier = jnp.cumsum(matches, axis=0) - matches
    position = jnp.sum(earlier * matches, axis=1)
    slot_of = jnp.where(alive > 0, target * capacity + position, -1)
    picked = (slot_of[None, :] == jnp.arange(slots, dtype=jnp.int32)[:, None]).astype(jnp.float32)
    payload = jnp.stack(
        [
            fractions[:, 0],
            fractions[:, 1],
            fractions[:, 2],
            charge,
            (cell_index // (span_y * K)).astype(jnp.float32),
            (cell_index // K % span_y).astype(jnp.float32),
            (cell_index % K).astype(jnp.float32),
            jnp.ones(charge.shape, jnp.float32),
        ],
        axis=1,
    )
    outgoing = jnp.dot(picked, payload.reshape(blocks, -1), precision=HIGHEST)
    outgoing = outgoing.reshape(cols_dev, capacity, 8, width)
    arrived = lax.all_to_all(outgoing, "py", split_axis=0, concat_axis=0, tiled=True)
    arrived = arrived.reshape(slots, 8, width)
    used = (arrived[:, 7, 0] > 0.5).astype(jnp.int32)
    place = jnp.where(used > 0, jnp.cumsum(used) - used, -1)
    chosen = (place[None, :] == jnp.arange(padded, dtype=jnp.int32)[:, None]).astype(jnp.float32)
    atoms = jnp.dot(chosen, arrived.reshape(slots, -1), precision=HIGHEST)
    batches = padded // SORT_BLOCKS
    members = SORT_BLOCKS * width
    atoms = (
        atoms.reshape(batches, SORT_BLOCKS, 8, width)
        .transpose(0, 2, 1, 3)
        .reshape(batches, 8, members)
    )
    number = jnp.arange(members, dtype=jnp.int32)
    key = jnp.where(atoms[:, 7] > 0.5, atoms[:, 4].astype(jnp.int32), K) * members + number
    rank = jnp.sum((key[:, None, :] < key[:, :, None]).astype(jnp.int32), axis=2)
    order = (rank[:, :, None] == number[None, None, :]).astype(jnp.float32)
    atoms = jnp.einsum("bcs,bsd->bcd", atoms, order, precision=HIGHEST)
    atoms = (
        atoms.reshape(batches, 8, members // (GROUP_BLOCKS * width), GROUP_BLOCKS * width)
        .transpose(0, 2, 1, 3)
        .reshape(groups, 8, GROUP_BLOCKS * width)
    )
    real = atoms[:, 7] > 0.5
    count = jnp.stack(
        [
            jnp.min(jnp.where(real, atoms[:, 4], 2.0 * K), axis=1),
            jnp.max(jnp.where(real, atoms[:, 4], -1.0 * K), axis=1),
        ]
    ).astype(jnp.int32)

    extended = deposit(count, atoms, rows, columns)
    moved_rows = from_behind(extended[span_x : span_x + 5], "px", 1)
    extended = jnp.concatenate([extended[:5] + moved_rows, extended[5:span_x]], axis=0)
    moved_cols = from_behind(extended[:, span_y : span_y + 5], "py", 1)
    grid = jnp.concatenate([extended[:, :5] + moved_cols, extended[:, 5:span_y]], axis=1)

    potential = transformed(
        grid.reshape(span_x * span_y, K), span_x, span_y, rows_dev, cols_dev
    ).reshape(span_x, span_y, K)
    lower_rows = from_behind(potential[:5], "px", -1)
    potential = jnp.concatenate([potential, lower_rows], axis=0)
    lower_cols = from_behind(potential[:, :5], "py", -1)
    potential = jnp.concatenate([potential, lower_cols], axis=1)
    potential = jnp.pad(
        potential, ((0, rows - span_x - 5), (0, columns - span_y - 5), (0, 0))
    )

    forces = pull(count, atoms, potential)[:, :3]
    forces = forces.reshape(batches, groups // batches, 3, -1).transpose(0, 2, 1, 3)
    forces = forces.reshape(batches, 3, members)
    forces = jnp.einsum("bcd,bsd->bcs", forces, order, precision=HIGHEST)
    forces = (
        forces.reshape(batches, 3, SORT_BLOCKS, width)
        .transpose(0, 2, 1, 3)
        .reshape(padded, 3 * width)
    )
    forces = lax.dot_general(chosen, forces, (((0,), (0,)), ((), ())), precision=HIGHEST)
    returned = lax.all_to_all(
        forces.reshape(cols_dev, capacity, 3, width), "py", split_axis=0, concat_axis=0, tiled=True
    ).reshape(slots, 3 * width)
    result = lax.dot_general(picked, returned, (((0,), (0,)), ((), ())), precision=HIGHEST)
    return result.reshape(blocks, 3, width)


def solution(mesh):
    split = (
        P(("px", "py"), None, None),
        P(("px", "py"), None),
        P(("px", "py"), None),
        P(("px", "py"), None),
        P(("px", "py")),
    )
    return jax.shard_map(
        per_device,
        mesh=mesh,
        in_specs=split,
        out_specs=P(("px", "py"), None, None),
        check_vma=False,
    )
```

```python
import math

import jax
import jax.numpy as jnp
import numpy as np
from jax import lax
from jax.experimental import pallas as pl
from jax.experimental.pallas import tpu as pltpu
from jax.sharding import PartitionSpec as P

K = 256
EWALD_GAIN = 4.0
EWALD_BETA = 0.6
SPLINE_SUMS = (1.0 / 120.0, 26.0 / 120.0, 66.0 / 120.0, 26.0 / 120.0, 1.0 / 120.0)
HIGHEST = lax.Precision.HIGHEST
HIGH = lax.Precision.HIGH
LANES = 128
ROWS_CHUNK = 10
SORT_BLOCKS = 8
GROUP_BLOCKS = 2


def hartley():
    steps = np.arange(K)
    angle = 2.0 * math.pi / K * (np.outer(steps, steps) % K)
    return (np.cos(angle) + np.sin(angle)).astype(np.float32)


def wave_profile():
    steps = np.arange(K)
    folded = np.where(2 * steps < K, steps, steps - K) / K
    waves = np.exp(2j * math.pi / K * np.outer(steps, np.arange(5)))
    modulus = 1.0 / np.abs(waves @ np.array(SPLINE_SUMS)) ** 2
    squared = folded * folded
    gauss = np.exp(-(math.pi * math.pi) * squared / (EWALD_BETA * EWALD_BETA))
    return squared.astype(np.float32), (gauss * modulus).astype(np.float32)


def from_behind(value, axis, steps):
    count = lax.axis_size(axis)
    pairs = [(source, (source + steps) % count) for source in range(count)]
    return lax.ppermute(value, axis, pairs)


def spline_six(u):
    older_values = [1.0 - u, u]
    slopes = []
    for spline_order in range(3, 7):
        newer_values = []
        for k in range(spline_order):
            terms = []
            if k >= 1:
                terms.append((u + (spline_order - 1 - k)) * older_values[k - 1])
            if k <= spline_order - 2:
                terms.append((k + 1 - u) * older_values[k])
            newer_values.append(sum(terms[1:], terms[0]) * (1.0 / (spline_order - 1)))
        if spline_order == 6:
            slopes = [-older_values[0]]
            slopes += [older_values[k - 1] - older_values[k] for k in range(1, 5)]
            slopes += [older_values[4]]
        older_values = newer_values
    return (older_values, slopes)


def placed(offset, values):
    table = jnp.zeros(offset.shape, jnp.float32)
    for k in range(6):
        table = jnp.where(offset == k, values[k], table)
    return table


def offsets(base, rows, wrap):
    width = base.shape[1]
    offset = lax.broadcasted_iota(jnp.int32, (rows, width), 0) - base
    return offset & (K - 1) if wrap else offset


def halves(value):
    upper = value.astype(jnp.bfloat16)
    lower = (value - upper.astype(jnp.float32)).astype(jnp.bfloat16)
    return upper, lower


def touched(span_ref, step, start):
    return (span_ref[0, step] < start + ROWS_CHUNK) & (span_ref[1, step] + 5 >= start)


def deposit_kernel(span_ref, atoms_ref, grid_ref):
    step = pl.program_id(0)
    rows, columns, depth = grid_ref.shape
    width = atoms_ref.shape[2]

    @pl.when(step == 0)
    def _():
        grid_ref[...] = jnp.zeros(grid_ref.shape, jnp.float32)

    @pl.when(span_ref[1, step] >= 0)
    def _():
        atoms = atoms_ref[0]
        base = atoms.astype(jnp.int32)
        table_x = placed(offsets(base[4:5], rows, False), spline_six(atoms[0:1])[0])
        table_y = placed(offsets(base[5:6], columns, False), spline_six(atoms[1:2])[0])
        table_z = placed(offsets(base[6:7], depth, True), spline_six(atoms[2:3])[0])
        upper, lower = halves((table_z * atoms[3:4]).T)
        weights = jnp.concatenate([upper, lower, upper], axis=0)
        for start in range(0, rows, ROWS_CHUNK):

            @pl.when(touched(span_ref, step, start))
            def _(start=start):
                chunk = table_x[start : start + ROWS_CHUNK]
                outer = (chunk[:, None, :] * table_y[None, :, :]).reshape(-1, width)
                upper, lower = halves(outer)
                spread = jnp.dot(
                    jnp.concatenate([upper, upper, lower], axis=1),
                    weights,
                    preferred_element_type=jnp.float32,
                )
                grid_ref[start : start + ROWS_CHUNK] += spread.reshape(-1, columns, depth)


def pull_kernel(span_ref, atoms_ref, potential_ref, forces_ref, parts, totals):
    step = pl.program_id(0)
    rows, columns, depth = potential_ref.shape
    width = atoms_ref.shape[2]
    piece = ROWS_CHUNK * columns

    @pl.when(step == 0)
    def _():
        for index in range(rows // ROWS_CHUNK):
            start = index * ROWS_CHUNK
            values = potential_ref[start : start + ROWS_CHUNK].reshape(piece, depth)
            upper, lower = halves(values)
            parts[index * piece : (index + 1) * piece] = jnp.concatenate(
                [upper, lower, upper], axis=1
            )

    @pl.when(span_ref[1, step] < 0)
    def _():
        forces_ref[...] = jnp.zeros(forces_ref.shape, jnp.float32)

    @pl.when(span_ref[1, step] >= 0)
    def _():
        atoms = atoms_ref[0]
        base = atoms.astype(jnp.int32)
        offset_x = offsets(base[4:5], rows, False)
        offset_y = offsets(base[5:6], columns, False)
        offset_z = offsets(base[6:7], depth, True)
        values, slopes = spline_six(atoms[0:1])
        table_x, slope_x = placed(offset_x, values), placed(offset_x, slopes)
        values, slopes = spline_six(atoms[1:2])
        table_y, slope_y = placed(offset_y, values), placed(offset_y, slopes)
        values, slopes = spline_six(atoms[2:3])
        both = jnp.concatenate([placed(offset_z, values), placed(offset_z, slopes)], axis=1)
        upper, lower = halves(both)
        weights = jnp.concatenate([upper, upper, lower], axis=0)
        totals[...] = jnp.zeros(totals.shape, jnp.float32)

        def folded(terms):
            return jnp.sum(terms.reshape(columns // 8, 8, width), axis=0)

        for index in range(rows // ROWS_CHUNK):

            @pl.when(touched(span_ref, step, index * ROWS_CHUNK))
            def _(index=index):
                start = index * ROWS_CHUNK
                sampled = jnp.dot(
                    parts[index * piece : (index + 1) * piece],
                    weights,
                    preferred_element_type=jnp.float32,
                ).reshape(ROWS_CHUNK, columns, 2 * width)
                sums = [totals[0], totals[1], totals[2]]
                for row in range(ROWS_CHUNK):
                    plain = sampled[row, :, :width]
                    sloped = sampled[row, :, width:]
                    value_x = table_x[start + row : start + row + 1]
                    turned_x = slope_x[start + row : start + row + 1]
                    sums[0] = sums[0] + turned_x * folded(plain * table_y)
                    sums[1] = sums[1] + value_x * folded(plain * slope_y)
                    sums[2] = sums[2] + value_x * folded(sloped * table_y)
                for axis in range(3):
                    totals[axis] = sums[axis]

        result = [-atoms[3:4] * jnp.sum(totals[axis], axis=0, keepdims=True) for axis in range(3)]
        forces_ref[0] = jnp.concatenate(
            result + [jnp.zeros((5, width), jnp.float32)], axis=0
        )


def deposit(count, atoms, rows, columns):
    groups, lines, width = atoms.shape
    return pl.pallas_call(
        deposit_kernel,
        out_shape=jax.ShapeDtypeStruct((rows, columns, K), jnp.float32),
        grid=(groups,),
        in_specs=[
            pl.BlockSpec(memory_space=pltpu.SMEM),
            pl.BlockSpec((1, lines, width), lambda g: (g, 0, 0)),
        ],
        out_specs=pl.BlockSpec((rows, columns, K), lambda g: (0, 0, 0)),
        compiler_params=pltpu.CompilerParams(vmem_limit_bytes=48 * 2**20),
        name="deposit",
    )(count, atoms)


def pull(count, atoms, potential):
    groups, lines, width = atoms.shape
    rows, columns, _ = potential.shape
    return pl.pallas_call(
        pull_kernel,
        out_shape=jax.ShapeDtypeStruct((groups, lines, width), jnp.float32),
        grid=(groups,),
        in_specs=[
            pl.BlockSpec(memory_space=pltpu.SMEM),
            pl.BlockSpec((1, lines, width), lambda g: (g, 0, 0)),
            pl.BlockSpec((rows, columns, K), lambda g: (0, 0, 0)),
        ],
        out_specs=pl.BlockSpec((1, lines, width), lambda g: (g, 0, 0)),
        scratch_shapes=[
            pltpu.VMEM((rows * columns, 3 * K), jnp.bfloat16),
            pltpu.VMEM((3, 8, width), jnp.float32),
        ],
        compiler_params=pltpu.CompilerParams(vmem_limit_bytes=48 * 2**20),
        name="pull",
    )(count, atoms, potential)


def exact_halves(values):
    upper = values.astype(jnp.bfloat16)
    return upper, (values - upper.astype(np.float32)).astype(jnp.bfloat16)


def product(left, right, transposed=False):
    dims = (((1,), (1 if transposed else 0,)), ((), ()))

    def one(a, b):
        return lax.dot_general(a, b, dims, preferred_element_type=jnp.float32)

    return one(left[0], right[0]) + (one(left[1], right[0]) + one(left[0], right[1]))


def convolve_kernel(
    counts,
    spectrum_ref,
    gain_ref,
    mix_upper,
    mix_lower,
    wave_upper,
    wave_lower,
    out_ref,
    columns_in,
    rows_out,
    rows_in,
    back_out,
    back_in,
    columns_out,
    send_sems,
    recv_sems,
    local_sems,
):
    chunks, step, bands = counts
    rows_dev = lax.axis_size("px")
    cols_dev = lax.axis_size("py")
    index_x = lax.axis_index("px")
    index_y = lax.axis_index("py")
    lines = step * bands
    packed = mix_upper.shape[1] // K
    span_x = packed * bands

    barrier = pltpu.get_barrier_semaphore()
    for axis, count, index in (("px", rows_dev, index_x), ("py", cols_dev, index_y)):
        for shift in range(1, count):
            pl.semaphore_signal(
                barrier,
                inc=1,
                device_id={axis: lax.rem(index + shift, count)},
                device_id_type=pl.DeviceIdType.MESH,
            )
    pl.semaphore_wait(barrier, rows_dev + cols_dev - 2)

    def exchange(stage, chunk, axis, source, target):
        count, index = (rows_dev, index_x) if axis == "px" else (cols_dev, index_y)
        copies = []
        for shift in range(1, count):
            peer = lax.rem(index + shift, count)
            copies.append(
                pltpu.make_async_remote_copy(
                    src_ref=source(peer),
                    dst_ref=target(index),
                    send_sem=send_sems.at[stage, chunk, shift],
                    recv_sem=recv_sems.at[stage, chunk, shift],
                    device_id={axis: peer},
                    device_id_type=pl.DeviceIdType.MESH,
                )
            )
        copies.append(
            pltpu.make_async_copy(source(index), target(index), local_sems.at[stage, chunk])
        )
        for copy in copies:
            copy.start()
        return copies

    def arrived(copies):
        for copy in copies[:-1]:
            copy.wait_recv()
        copies[-1].wait()

    def lanes(index):
        return pl.ds(pl.multiple_of(index * LANES, LANES), LANES)

    def band_rows(index):
        return pl.ds(pl.multiple_of(index * span_x, span_x), span_x)

    started = []
    first, second, third, fourth = [], [], [], []
    for h in range(chunks):
        part = pl.ds(h * lines, lines)
        first.append(
            exchange(
                0,
                h,
                "py",
                lambda peer: spectrum_ref.at[peer, :, part],
                lambda index: columns_in.at[h, :, :, lanes(index)],
            )
        )
    for h in range(chunks):
        arrived(first[h])
        values = columns_in[h].reshape(rows_dev * lines, cols_dev * LANES)
        mixed = product(halves(values), (mix_upper[...], mix_lower[...]))
        for r in range(rows_dev):
            for j in range(step):
                start = r * lines + j * bands
                for p in range(packed):
                    rows_out[h, r, j, p * bands : (p + 1) * bands, :] = mixed[
                        start : start + bands, p * K : (p + 1) * K
                    ]
        second.append(
            exchange(
                1,
                h,
                "px",
                lambda peer: rows_out.at[h, peer],
                lambda index: rows_in.at[h, :, band_rows(index)],
            )
        )
    for h in range(chunks):
        arrived(second[h])
        wave = (wave_upper[...], wave_lower[...])
        for j in range(step):
            mixed = product(wave, halves(rows_in[h, j])) * gain_ref[h * step + j]
            back_out[h, j] = product(wave, halves(mixed))
        third.append(
            exchange(
                2,
                h,
                "px",
                lambda peer: back_out.at[h, :, band_rows(peer)],
                lambda index: back_in.at[h, index],
            )
        )
    for h in range(chunks):
        arrived(third[h])
        values = jnp.concatenate(
            [
                jnp.concatenate(
                    [back_in[h, r, j, p * bands : (p + 1) * bands, :] for p in range(packed)],
                    axis=1,
                )
                for r in range(rows_dev)
                for j in range(step)
            ],
            axis=0,
        )
        mixed = product(halves(values), (mix_upper[...], mix_lower[...]), transposed=True)
        columns_out[h] = mixed.reshape(rows_dev, lines, cols_dev * LANES)
        part = pl.ds(h * lines, lines)
        fourth.append(
            exchange(
                3,
                h,
                "py",
                lambda peer: columns_out.at[h, :, :, lanes(peer)],
                lambda index: out_ref.at[index, :, part],
            )
        )
    for h in range(chunks):
        arrived(fourth[h])
    for stage in (first, second, third, fourth):
        for copies in stage:
            for copy in copies[:-1]:
                copy.wait_send()


def convolve(spectrum, gain, mixing, matrix, bands):
    cols_dev, rows_dev, held, _ = spectrum.shape
    slab = held // bands
    chunks = 4
    while slab % chunks or (slab // chunks * bands) % 8:
        chunks //= 2
    step = slab // chunks
    lines = step * bands
    span_x = K // rows_dev
    peers = max(rows_dev, cols_dev)
    mix_upper, mix_lower = exact_halves(mixing)
    wave_upper, wave_lower = exact_halves(matrix)
    columns_shape = (chunks, rows_dev, lines, cols_dev * LANES)
    rows_shape = (chunks, rows_dev, step, span_x, K)
    full_shape = (chunks, step, K, K)

    def body(*refs):
        convolve_kernel((chunks, step, bands), *refs)

    whole = pl.BlockSpec(memory_space=pltpu.VMEM)
    return pl.pallas_call(
        body,
        out_shape=jax.ShapeDtypeStruct(spectrum.shape, jnp.float32),
        in_specs=[whole] * 6,
        out_specs=whole,
        scratch_shapes=[
            pltpu.VMEM(columns_shape, jnp.float32),
            pltpu.VMEM(rows_shape, jnp.float32),
            pltpu.VMEM(full_shape, jnp.float32),
            pltpu.VMEM(full_shape, jnp.float32),
            pltpu.VMEM(rows_shape, jnp.float32),
            pltpu.VMEM(columns_shape, jnp.float32),
            pltpu.SemaphoreType.DMA((4, chunks, peers)),
            pltpu.SemaphoreType.DMA((4, chunks, peers)),
            pltpu.SemaphoreType.DMA((4, chunks)),
        ],
        compiler_params=pltpu.CompilerParams(
            collective_id=0, has_side_effects=True, vmem_limit_bytes=56 * 2**20
        ),
        name="convolve",
    )(
        spectrum,
        gain,
        jnp.asarray(mix_upper),
        jnp.asarray(mix_lower),
        jnp.asarray(wave_upper),
        jnp.asarray(wave_lower),
    )


def transformed(grid, span_x, span_y, rows_dev, cols_dev):
    table = hartley()
    matrix = jnp.asarray(table)
    packed = LANES // span_y
    bands = span_x // packed
    span_z = K // cols_dev
    slab = span_z // rows_dev
    mixing = np.einsum("syk,pq->spyqk", table.reshape(cols_dev, span_y, K), np.eye(packed))
    mixing = mixing.reshape(cols_dev * LANES, packed * K).astype(np.float32)

    squared, profile = (jnp.asarray(values) for values in wave_profile())
    first = lax.axis_index("py") * span_z + lax.axis_index("px") * slab
    squared_z = lax.dynamic_slice(squared, (first,), (slab,))
    profile_z = lax.dynamic_slice(profile, (first,), (slab,))
    total = squared_z[:, None, None] + squared[None, :, None] + squared[None, None, :]
    gain = profile_z[:, None, None] * profile[None, :, None] * profile[None, None, :]
    gain = jnp.where(
        total > 0, (EWALD_GAIN / float(K**3)) * gain / jnp.where(total > 0, total, 1.0), 0.0
    )

    ordered = grid.reshape(packed, bands, span_y, K).transpose(1, 0, 2, 3).reshape(-1, K)
    spectrum = lax.dot_general(matrix, ordered, (((1,), (1,)), ((), ())), precision=HIGH)
    spectrum = spectrum.reshape(cols_dev, rows_dev, slab * bands, LANES)
    spectrum = convolve(spectrum, gain, mixing, table, bands)
    spectrum = spectrum.reshape(K, span_x * span_y)
    ordered = lax.dot_general(spectrum, matrix, (((0,), (0,)), ((), ())), precision=HIGH)
    return ordered.reshape(bands, packed, span_y, K).transpose(1, 0, 2, 3)


def permuted(form, values, order):
    parts = []
    for _ in range(3):
        part = lax.reduce_precision(values, exponent_bits=8, mantissa_bits=7)
        parts.append(part.astype(jnp.bfloat16))
        values = values - part
    moved = jnp.einsum(
        form, jnp.concatenate(parts, axis=1), order, preferred_element_type=jnp.float32
    )
    upper, middle, lower = jnp.split(moved, 3, axis=1)
    return (upper + middle) + lower


def per_device(fractions, charge, cell_index, destination, live_blocks):
    rows_dev = lax.axis_size("px")
    cols_dev = lax.axis_size("py")
    span_x = K // rows_dev
    span_y = K // cols_dev
    blocks, width = charge.shape
    capacity = max(2, 3 * blocks // (2 * cols_dev))
    slots = cols_dev * capacity
    padded = -(-slots // SORT_BLOCKS) * SORT_BLOCKS
    groups = padded // GROUP_BLOCKS
    rows = -(-(span_x + 5) // ROWS_CHUNK) * ROWS_CHUNK
    columns = -(-(span_y + 5) // 8) * 8

    alive = (jnp.arange(blocks, dtype=jnp.int32) < live_blocks[0]).astype(jnp.int32)
    target = destination[:, 0]
    matches = (target[:, None] == jnp.arange(cols_dev, dtype=jnp.int32)[None, :]).astype(jnp.int32)
    matches = matches * alive[:, None]
    earlier = jnp.cumsum(matches, axis=0) - matches
    position = jnp.sum(earlier * matches, axis=1)
    slot_of = jnp.where(alive > 0, target * capacity + position, -1)
    picked = (slot_of[None, :] == jnp.arange(slots, dtype=jnp.int32)[:, None]).astype(jnp.float32)
    payload = jnp.stack(
        [
            fractions[:, 0],
            fractions[:, 1],
            fractions[:, 2],
            charge,
            (cell_index // (span_y * K)).astype(jnp.float32),
            (cell_index // K % span_y).astype(jnp.float32),
            (cell_index % K).astype(jnp.float32),
            jnp.ones(charge.shape, jnp.float32),
        ],
        axis=1,
    )
    outgoing = jnp.dot(picked, payload.reshape(blocks, -1), precision=HIGHEST)
    outgoing = outgoing.reshape(cols_dev, capacity, 8, width)
    arrived = lax.all_to_all(outgoing, "py", split_axis=0, concat_axis=0, tiled=True)
    arrived = arrived.reshape(slots, 8, width)
    used = (arrived[:, 7, 0] > 0.5).astype(jnp.int32)
    place = jnp.where(used > 0, jnp.cumsum(used) - used, -1)
    chosen = (place[None, :] == jnp.arange(padded, dtype=jnp.int32)[:, None]).astype(jnp.float32)
    atoms = jnp.dot(chosen, arrived.reshape(slots, -1), precision=HIGHEST)
    batches = padded // SORT_BLOCKS
    members = SORT_BLOCKS * width
    atoms = (
        atoms.reshape(batches, SORT_BLOCKS, 8, width)
        .transpose(0, 2, 1, 3)
        .reshape(batches, 8, members)
    )
    number = jnp.arange(members, dtype=jnp.int32)
    key = jnp.where(atoms[:, 7] > 0.5, atoms[:, 4].astype(jnp.int32), K) * members + number
    rank = jnp.sum((key[:, None, :] < key[:, :, None]).astype(jnp.int32), axis=2)
    order = (rank[:, :, None] == number[None, None, :]).astype(jnp.bfloat16)
    atoms = permuted("bcs,bsd->bcd", atoms, order)
    atoms = (
        atoms.reshape(batches, 8, members // (GROUP_BLOCKS * width), GROUP_BLOCKS * width)
        .transpose(0, 2, 1, 3)
        .reshape(groups, 8, GROUP_BLOCKS * width)
    )
    real = atoms[:, 7] > 0.5
    count = jnp.stack(
        [
            jnp.min(jnp.where(real, atoms[:, 4], 2.0 * K), axis=1),
            jnp.max(jnp.where(real, atoms[:, 4], -1.0 * K), axis=1),
        ]
    ).astype(jnp.int32)

    extended = deposit(count, atoms, rows, columns)
    moved_rows = from_behind(extended[span_x : span_x + 5], "px", 1)
    extended = jnp.concatenate([extended[:5] + moved_rows, extended[5:span_x]], axis=0)
    moved_cols = from_behind(extended[:, span_y : span_y + 5], "py", 1)
    grid = jnp.concatenate([extended[:, :5] + moved_cols, extended[:, 5:span_y]], axis=1)

    potential = transformed(
        grid.reshape(span_x * span_y, K), span_x, span_y, rows_dev, cols_dev
    ).reshape(span_x, span_y, K)
    lower_rows = from_behind(potential[:5], "px", -1)
    potential = jnp.concatenate([potential, lower_rows], axis=0)
    lower_cols = from_behind(potential[:, :5], "py", -1)
    potential = jnp.concatenate([potential, lower_cols], axis=1)
    potential = jnp.pad(
        potential, ((0, rows - span_x - 5), (0, columns - span_y - 5), (0, 0))
    )

    forces = pull(count, atoms, potential)[:, :3]
    forces = forces.reshape(batches, groups // batches, 3, -1).transpose(0, 2, 1, 3)
    forces = forces.reshape(batches, 3, members)
    forces = permuted("bcd,bsd->bcs", forces, order)
    forces = (
        forces.reshape(batches, 3, SORT_BLOCKS, width)
        .transpose(0, 2, 1, 3)
        .reshape(padded, 3 * width)
    )
    forces = lax.dot_general(chosen, forces, (((0,), (0,)), ((), ())), precision=HIGHEST)
    returned = lax.all_to_all(
        forces.reshape(cols_dev, capacity, 3, width), "py", split_axis=0, concat_axis=0, tiled=True
    ).reshape(slots, 3 * width)
    result = lax.dot_general(picked, returned, (((0,), (0,)), ((), ())), precision=HIGHEST)
    return result.reshape(blocks, 3, width)


def solution(mesh):
    split = (
        P(("px", "py"), None, None),
        P(("px", "py"), None),
        P(("px", "py"), None),
        P(("px", "py"), None),
        P(("px", "py")),
    )
    return jax.shard_map(
        per_device,
        mesh=mesh,
        in_specs=split,
        out_specs=P(("px", "py"), None, None),
        check_vma=False,
    )
```
